32 devices in a mesh: groups: 2 (over x), ctx: 16 (over z, y, core).
Axes of the slice: x: 2, y: 2, z: 4, core: 2. Of those that a mesh axis runs over, the one named last changes fastest.
Arguments:
- queries: bfloat16 [4096, 768], P(('groups', 'ctx')), parts along dimension 0, may hold values from -80 to 80
- keys: bfloat16 [4096, 128], P(('groups', 'ctx')), parts along dimension 0, may hold values from -4 to 4
- values: bfloat16 [4096, 128], P(('groups', 'ctx')), parts along dimension 0, may hold values from -5 to 5
- out_grad: bfloat16 [4096, 768], P(('groups', 'ctx')), parts along dimension 0, may hold values from -5 to 5
- segment_ids: int32 [4096], P(('groups', 'ctx')), parts along dimension 0, may hold values from 0 to 5, never falling along the last dimension, each value on 1 to 512 neighbouring positions
- route: int32 [32, 16], P(('groups', 'ctx')), parts along dimension 0, may hold values from 0 to 15, each once within a row
Outputs:
- attended: bfloat16 [4096, 768], P(('groups', 'ctx')), parts along dimension 0
- query_grad: bfloat16 [4096, 768], P(('groups', 'ctx')), parts along dimension 0
- key_grad: bfloat16 [4096, 128], P(('groups', 'ctx')), parts along dimension 0
- value_grad: bfloat16 [4096, 128], P(('groups', 'ctx')), parts along dimension 0
The draws below stay inside these ranges and needn't reach their ends.
There are 2 independent parts, one for each index of `groups`. The reference program is written for one: setup_inputs(seed, part) draws one part's arguments, and reference() takes and returns one part's arrays. A program takes and returns all parts, laid end to end along the dimension named above; each array names one. Nothing has to cross between parts.
Inputs may be any that keep to these rules, and one draw needn't show every extreme that they name: `segment_ids`: never falling along the pack; segment s belongs to DPO example s // 3 as its prompt (s % 3 == 0), chosen (1) or rejected (2) answer; each segment holds 1 to 512 tokens, one exactly that many. `route`: each row holds every number of its range once.
All inputs are finite; a program needn't handle non-finite values.
Results may differ from the reference program's by a relative error of at most 0.012.
The reference program's roundings to bfloat16 on the way (of `prob_low`, `attended_rows`, `grad_score` and `query_grad_rows`) count: a program that leaves them out, or rounds other values in their place, can miss the bound.
Values may be sent and summed in bfloat16 or wider, within the bound.
A program may use at most 64 MiB of HBM per device.

```python
import math
import jax
import jax.numpy as jnp
import numpy as np
from jax import lax

DH = 128
HQ = 6
TOK_DEV = 128
TOKENS = 2048
SUB = 8
EXAMPLES = 2
N_CTX = 16


def draw_keys(key, part):
    key = jax.random.fold_in(key, 7)
    return jnp.clip(jax.random.normal(key, (TOKENS, DH), jnp.float32), -4.0, 4.0).astype(jnp.bfloat16)


def draw_queries(key, part):
    key = jax.random.fold_in(key, 9)
    return jnp.clip(jax.random.normal(key, (TOKENS, HQ * DH), jnp.float32), -4.0, 4.0).astype(jnp.bfloat16)


def level_of(key, dims, shards, low, high):
    loudness = 1.0
    for dim, parts in shards:
        steps = jax.random.uniform(jax.random.fold_in(jax.random.fold_in(key, 6), dim), (parts,), jnp.float32, low / len(shards), high / len(shards))
        loudness = loudness * jnp.repeat(jnp.exp(steps), dims[dim] // parts).reshape((-1,) + (1,) * (len(dims) - 1 - dim))
    return loudness


def length_profile(count, total, bound, lean):
    loads = [(1 << 20) // math.isqrt(standing ** lean) + 1 for standing in range(2, count + 1)]
    surplus, given = total - bound - (count - 1), [1] * (count - 1)
    while surplus > 0:
        free = [i for i in range(count - 1) if given[i] < bound]
        pool, left = sum([loads[i] for i in free]), surplus
        for i in free:
            more = min(bound - given[i], max(1, left * loads[i] // pool), surplus)
            given[i] = given[i] + more
            surplus = surplus - more
    return np.array([bound] + given)


def uneven(stream_key, count, total, reach, lean):
    if count == 2:
        one = jax.random.randint(stream_key, (), max(1, total - reach), min(reach, total - 1) + 1)
        return jnp.stack([one, total - one])
    lengths = jnp.asarray(length_profile(count, total, reach, lean), jnp.int32)
    pairs = (count - 1) // 2
    source_of, receiver = lengths[1:1 + 2 * pairs:2], lengths[2:2 + 2 * pairs:2]
    room = jnp.minimum(source_of - 1, reach - receiver)
    passed = jax.random.randint(jax.random.fold_in(stream_key, 1), (pairs,), 0, 1 << 20) % (room + 1)
    lengths = lengths.at[1:1 + 2 * pairs:2].set(source_of - passed).at[2:2 + 2 * pairs:2].set(receiver + passed)
    return lengths[jax.random.permutation(jax.random.fold_in(stream_key, 2), count)]


def gaussian(own_key, extent, scale, bound, pieces=(), held_as=jnp.bfloat16):
    level = level_of(own_key, extent, pieces, -0.22, 0.18) if pieces else 1.0
    drawn = jax.random.normal(own_key, extent, jnp.float32) * scale * level
    return jnp.minimum(jnp.maximum(drawn, -bound), bound).astype(held_as)


def setup_inputs(seed: int = 0, part: int = 0) -> dict:
    splits = jax.random.split(jax.random.key(seed), 7)
    own_keys = jax.random.split(jax.random.fold_in(splits[6], part), 7)
    queries = draw_queries(jax.random.fold_in(jax.random.fold_in(splits[6], part), 71), part)
    keys = draw_keys(jax.random.fold_in(jax.random.fold_in(splits[6], part), 71), part)
    values = gaussian(own_keys[2], (TOKENS, DH), 1.0, 5.0, ((0, 16),))
    out_grad = gaussian(own_keys[3], (TOKENS, HQ * DH), 1.0, 5.0, ((0, 16),))
    segment_ids = jnp.searchsorted(jnp.cumsum(uneven(own_keys[4], 3 * EXAMPLES, TOKENS, 4 * TOK_DEV, 1)), jnp.arange(TOKENS), side="right").astype(jnp.int32)
    route = jax.vmap(lambda own: jax.random.permutation(own, N_CTX))(jax.random.split(own_keys[5], N_CTX)).reshape((N_CTX, N_CTX)).astype(jnp.int32)
    return dict(queries=queries, keys=keys, values=values, out_grad=out_grad, segment_ids=segment_ids, route=route)


def reference(queries, keys, values, out_grad, segment_ids, route):
    factor = DH ** -0.5
    position = jnp.arange(TOKENS, dtype=jnp.int32)
    example = segment_ids // 3
    segment_role = segment_ids % 3
    allowed = (position[None, :] <= position[:, None]) & (example[None, :] == example[:, None]) & ((segment_role[None, :] == segment_role[:, None]) | (segment_role[None, :] == 0))

    def one_head(head):
        query_head = lax.dynamic_slice_in_dim(queries, head * DH, DH, 1)
        grad_head = lax.dynamic_slice_in_dim(out_grad, head * DH, DH, 1)
        scores = jnp.dot(query_head, keys.T, preferred_element_type=jnp.float32) * factor
        scores = jnp.where(allowed, scores, -jnp.inf)
        row_top = jnp.max(scores, axis=1, keepdims=True)
        log_total = row_top + jnp.log(jnp.sum(jnp.exp(scores - row_top), axis=1, keepdims=True))
        attn_prob = jnp.exp(scores - log_total)
        prob_low = attn_prob.astype(jnp.bfloat16)
        attended = jnp.dot(prob_low, values, preferred_element_type=jnp.float32).astype(jnp.bfloat16)
        row_dots = jnp.sum(grad_head.astype(jnp.float32) * attended.astype(jnp.float32), axis=1, keepdims=True)
        value_grad = jnp.dot(prob_low.T, grad_head, preferred_element_type=jnp.float32)
        grad_prob = jnp.dot(grad_head, values.T, preferred_element_type=jnp.float32)
        grad_score = (attn_prob * (grad_prob - row_dots)).astype(jnp.bfloat16)
        query_grad = (jnp.dot(grad_score, keys, preferred_element_type=jnp.float32) * factor).astype(jnp.bfloat16)
        key_grad = jnp.dot(grad_score.T, query_head, preferred_element_type=jnp.float32) * factor
        return attended, query_grad, key_grad, value_grad

    attended, query_grad, key_grad, value_grad = lax.map(one_head, jnp.arange(HQ, dtype=jnp.int32))
    attended_rows = attended.transpose(1, 0, 2).reshape(TOKENS, HQ * DH)
    query_grad_rows = query_grad.transpose(1, 0, 2).reshape(TOKENS, HQ * DH)
    owner_rows = (jnp.arange(N_CTX, dtype=jnp.int32)[None, :, None] * TOK_DEV + route.T[:, :, None] * SUB + jnp.arange(SUB, dtype=jnp.int32)[None, None, :]).reshape(TOKENS)
    return (attended_rows[owner_rows], query_grad_rows[owner_rows], jnp.sum(key_grad, axis=0).astype(jnp.bfloat16), jnp.sum(value_grad, axis=0).astype(jnp.bfloat16))
```

```python
import functools

import jax
import jax.numpy as jnp
from jax import lax
from jax.experimental import pallas as pl
from jax.experimental.pallas import tpu as pltpu
from jax.sharding import PartitionSpec as P

MESH = pl.DeviceIdType.MESH
F32 = jnp.float32
BF16 = jnp.bfloat16
big_negative = -1e30
reach = 3 * 512
pad_rows = 8
LANES = 256


def flip(block):
    return block.astype(F32).T.astype(BF16)


def product(left, right):
    return jnp.dot(left, right, preferred_element_type=F32)


def kernel(
    n, heads, factor, back, sub,
    q_ref, k_ref, v_ref, g_ref, seg_ref, route_ref,
    att_ref, dq_ref, kg_ref, vg_ref,
    kv, q_t, g_t, q_rows, g_rows, perm, score, prob, grad_score, top, total, out_t, dq_t,
    half_terms, own_terms, sib_out, sib_in, part_out, part_in, att_out, dq_out, att_in, dq_in,
    kv_send, kv_recv, fwd_send, fwd_recv, sib_send, sib_recv, part_send, part_recv,
    att_send, att_recv, dq_send, dq_recv,
):
    me = lax.axis_index("ctx")
    chip, core = lax.div(me, 2), lax.rem(me, 2)
    other = 1 - core
    sibling = chip * 2 + other
    chips = n // 2
    rows, dh = k_ref.shape
    columns = heads * rows
    far = jnp.minimum(chip, back)
    ahead = jnp.minimum(chips - 1 - chip, back)

    barrier = pltpu.get_barrier_semaphore()

    def greet(step, carry):
        pl.semaphore_signal(
            barrier, inc=1, device_id={"ctx": lax.rem(me + step, n)}, device_id_type=MESH
        )
        return carry

    lax.fori_loop(1, n, greet, 0)

    own_seg = seg_ref[...].astype(F32)
    kv[0, core, pl.ds(0, rows), :] = k_ref[...]
    kv[0, core, pl.ds(rows, rows), :] = v_ref[...]
    kv[0, core, pl.ds(2 * rows, 16), :] = jnp.broadcast_to(own_seg, (16, rows)).astype(BF16)
    pl.semaphore_wait(barrier, n - 1)

    def kv_copy(step, target):
        return pltpu.make_async_remote_copy(
            src_ref=kv.at[0, core], dst_ref=kv.at[step, core],
            send_sem=kv_send.at[step], recv_sem=kv_recv.at[step],
            device_id={"ctx": target}, device_id_type=MESH,
        )

    def fwd_copy(step, which):
        return pltpu.make_async_remote_copy(
            src_ref=kv.at[step, which], dst_ref=kv.at[step, which],
            send_sem=fwd_send.at[step], recv_sem=fwd_recv.at[step],
            device_id={"ctx": sibling}, device_id_type=MESH,
        )

    def sib_copy(step):
        return pltpu.make_async_remote_copy(
            src_ref=sib_out.at[step], dst_ref=sib_in.at[step],
            send_sem=sib_send.at[step], recv_sem=sib_recv.at[step],
            device_id={"ctx": sibling}, device_id_type=MESH,
        )

    def part_copy(step, target):
        return pltpu.make_async_remote_copy(
            src_ref=part_out.at[step], dst_ref=part_in.at[step],
            send_sem=part_send.at[step], recv_sem=part_recv.at[step],
            device_id={"ctx": target}, device_id_type=MESH,
        )

    def row_copy(outgoing, incoming, sends, recvs, step):
        target = lax.rem(me + step, n)
        return pltpu.make_async_remote_copy(
            src_ref=outgoing.at[target], dst_ref=incoming.at[me],
            send_sem=sends.at[step], recv_sem=recvs.at[step],
            device_id={"ctx": target}, device_id_type=MESH,
        )

    fwd_copy(0, core).start()

    def send_kv(step, carry):
        kv_copy(step, me + 2 * step).start()
        return carry

    lax.fori_loop(1, ahead + 1, send_kv, 0)

    for h in range(heads):
        part = slice(h * dh, (h + 1) * dh)
        block = slice(h * rows, (h + 1) * rows)
        q_h, g_h = q_ref[:, part], g_ref[:, part]
        q_t[:, block] = flip(q_h)
        g_t[:, block] = flip(g_h)
        q_rows[block, :] = q_h
        g_rows[block, :] = g_h

    slots = n * pad_rows
    spread = (
        lax.shift_right_logical(lax.broadcasted_iota(jnp.int32, (n, slots), 1), 3)
        == lax.broadcasted_iota(jnp.int32, (n, slots), 0)
    )
    routing = jnp.broadcast_to(route_ref[...].astype(F32), (16, n)).astype(BF16)
    block_of = product(routing, jnp.where(spread, 1.0, 0.0).astype(BF16))[:1]
    token = lax.broadcasted_iota(jnp.int32, (rows, slots), 1) & (pad_rows - 1)
    wanted = block_of * float(sub) + token.astype(F32)
    chosen = (wanted == lax.broadcasted_iota(jnp.int32, (rows, slots), 0).astype(F32)) & (token < sub)
    perm[...] = jnp.where(chosen, 1.0, 0.0).T.astype(BF16)

    top[...] = jnp.full_like(top, big_negative)
    prompt = jnp.floor((own_seg + 0.5) * (1.0 / 3.0)) * 3.0
    query_pos = lax.broadcasted_iota(jnp.int32, (rows, rows), 1) + core * rows
    key_row = lax.broadcasted_iota(jnp.int32, (rows, rows), 0)
    chunks = [slice(at, at + LANES) for at in range(0, columns, LANES)]

    def score_half(step, half):
        key_block = kv[step, half, pl.ds(0, rows), :]
        seg_tile = kv[step, half, pl.ds(2 * rows, 16), :].astype(F32)
        key_seg = jnp.broadcast_to(seg_tile[:1], (rows, rows)).T
        key_pos = key_row + (half * rows - step * 2 * rows)
        allowed = (key_pos <= query_pos) & ((key_seg == own_seg) | (key_seg == prompt))
        bias = jnp.where(allowed, 0.0, big_negative)
        bias = jnp.concatenate([bias] * (LANES // rows), axis=1)
        at = pl.ds(pl.multiple_of(half * rows, rows), rows)
        for chunk in chunks:
            values = product(key_block, q_t[:, chunk]) * factor + bias
            score[step, at, chunk] = values
            top[:, chunk] = jnp.maximum(
                top[:, chunk], jnp.max(values.reshape(rows // 8, 8, LANES), axis=0)
            )

    def scores(step, carry):
        @pl.when(step > 0)
        def _():
            kv_copy(step, me).wait_recv()
            fwd_copy(step, core).start()

        score_half(step, core)
        fwd_copy(step, other).wait_recv()
        score_half(step, other)
        return carry

    lax.fori_loop(0, far + 1, scores, 0)
    row_top = jnp.max(top[...], axis=0, keepdims=True)
    top[...] = jnp.broadcast_to(row_top, top.shape)
    total[...] = jnp.zeros_like(total)
    out_t[...] = jnp.zeros_like(out_t)
    dq_t[...] = jnp.zeros_like(dq_t)

    def sums(step, carry):
        for at in (pl.ds(0, rows), pl.ds(rows, rows)):
            for chunk in chunks:
                values = jnp.exp(score[step, at, chunk] - top[:1, chunk])
                score[step, at, chunk] = values
                total[:, chunk] += jnp.sum(values.reshape(rows // 8, 8, LANES), axis=0)
        return carry

    lax.fori_loop(0, far + 1, sums, 0)
    total[...] = jnp.broadcast_to(
        1.0 / jnp.sum(total[...], axis=0, keepdims=True), total.shape
    )

    def both(step, first):
        return jnp.concatenate(
            [kv[step, 0, pl.ds(first, rows), :], kv[step, 1, pl.ds(first, rows), :]], axis=0
        )

    def outputs(step, carry):
        value_t = flip(both(step, rows))
        for chunk in chunks:
            values = score[step, :, chunk] * total[:1, chunk]
            score[step, :, chunk] = values
            low = values.astype(BF16)
            prob[step, :, chunk] = low
            out_t[:, chunk] += product(value_t, low)
        return carry

    lax.fori_loop(0, far + 1, outputs, 0)

    def stage(transposed, outgoing, incoming, sends, recvs):
        pieces = []
        for h in range(heads):
            low = transposed[:, h * rows:(h + 1) * rows].astype(BF16)
            moved = lax.dot_general(
                perm[...], low, (((1,), (1,)), ((), ())), preferred_element_type=F32
            )
            pieces.append(moved.reshape(n, pad_rows, dh))
        for h in range(0, heads, 2):
            outgoing[:, h * pad_rows:(h + 2) * pad_rows, :] = jnp.concatenate(
                pieces[h:h + 2], axis=1
            ).astype(BF16)

        def send(step, carry):
            row_copy(outgoing, incoming, sends, recvs, step).start()
            return carry

        lax.fori_loop(1, n, send, 0)
        incoming[me] = outgoing[me]

    stage(out_t, att_out, att_in, att_send, att_recv)
    for chunk in chunks:
        low = out_t[:, chunk].astype(BF16).astype(F32)
        dots = jnp.sum(g_t[:, chunk].astype(F32) * low, axis=0, keepdims=True)
        top[:, chunk] = jnp.broadcast_to(dots, (8, LANES))

    def finish(step):
        sib_copy(step).wait_recv()
        own_terms[step] = own_terms[step] + sib_in[step].astype(F32)

        @pl.when(step > 0)
        def _():
            part_out[step] = own_terms[step].astype(BF16)
            part_copy(step, me - 2 * step).start()

    def grads(turn, carry):
        step = far - turn
        value_block, key_t = both(step, rows), flip(both(step, 0))
        for chunk in chunks:
            grad_prob = product(value_block, g_t[:, chunk])
            low = (score[step, :, chunk] * (grad_prob - top[:1, chunk])).astype(BF16)
            grad_score[:, chunk] = low
            dq_t[:, chunk] += product(key_t, low)
        key_part = product(grad_score[...], q_rows[...])
        value_part = product(prob[step], g_rows[...])
        for half in range(2):
            part = slice(half * rows, (half + 1) * rows)
            half_terms[half, :rows] = key_part[part]
            half_terms[half, rows:] = value_part[part]
        sib_out[step] = half_terms[other].astype(BF16)
        sib_copy(step).start()
        own_terms[step] = half_terms[core]

        @pl.when(turn > 0)
        def _():
            finish(step + 1)

        return carry

    lax.fori_loop(0, far + 1, grads, 0)
    dq_t[...] = dq_t[...] * factor
    stage(dq_t, dq_out, dq_in, dq_send, dq_recv)
    finish(0)

    def collect(incoming, outgoing, sends, recvs, result):
        def arrive(step, carry):
            row_copy(outgoing, incoming, sends, recvs, step).wait_recv()
            return carry

        lax.fori_loop(1, n, arrive, 0)
        if sub == pad_rows:
            for h in range(0, heads, 2):
                two = incoming[:, h * pad_rows:(h + 2) * pad_rows, :].astype(F32)
                for one in range(2):
                    result[:, (h + one) * dh:(h + one + 1) * dh] = (
                        two[:, one * pad_rows:(one + 1) * pad_rows]
                        .reshape(n * pad_rows, dh)
                        .astype(BF16)
                    )
        else:
            result[...] = incoming[...]

        def sent(step, carry):
            row_copy(outgoing, incoming, sends, recvs, step).wait_send()
            return carry

        lax.fori_loop(1, n, sent, 0)

    collect(att_in, att_out, att_send, att_recv, att_ref)

    def gather_part(step, carry):
        part_copy(step, me).wait_recv()
        own_terms[0] = own_terms[0] + part_in[step].astype(F32)
        return carry

    lax.fori_loop(1, ahead + 1, gather_part, 0)
    kg_ref[...] = (own_terms[0, :rows] * factor).astype(BF16)
    vg_ref[...] = own_terms[0, rows:].astype(BF16)
    collect(dq_in, dq_out, dq_send, dq_recv, dq_ref)

    def drain(step, carry):
        fwd_copy(step, core).wait_send()
        sib_copy(step).wait_send()
        return carry

    lax.fori_loop(0, far + 1, drain, 0)

    def drain_kv(step, carry):
        kv_copy(step, me).wait_send()
        return carry

    lax.fori_loop(1, ahead + 1, drain_kv, 0)

    def drain_parts(step, carry):
        part_copy(step, me).wait_send()
        return carry

    lax.fori_loop(1, far + 1, drain_parts, 0)


def body(n, queries, keys, values, out_grad, segment_ids, route):
    rows, dh = keys.shape
    heads = queries.shape[1] // dh
    sub = rows // n
    chips = n // 2
    back = min(-(-(reach - 1) // (2 * rows)), chips - 1)
    columns = heads * rows
    held = back + 1
    slots = n * pad_rows
    moved = (n, heads * pad_rows, dh)
    row_shape = queries.shape if sub == pad_rows else moved
    vmem = pl.BlockSpec(memory_space=pltpu.VMEM)
    dma = pltpu.SemaphoreType.DMA
    attended, query_grad, key_grad, value_grad = pl.pallas_call(
        functools.partial(kernel, n, heads, dh ** -0.5, back, sub),
        out_shape=(
            jax.ShapeDtypeStruct(row_shape, BF16),
            jax.ShapeDtypeStruct(row_shape, BF16),
            jax.ShapeDtypeStruct((rows, dh), BF16),
            jax.ShapeDtypeStruct((rows, dh), BF16),
        ),
        in_specs=[vmem] * 6,
        out_specs=(vmem,) * 4,
        scratch_shapes=[
            pltpu.VMEM((held, 2, 2 * rows + 16, dh), BF16),
            pltpu.VMEM((dh, columns), BF16),
            pltpu.VMEM((dh, columns), BF16),
            pltpu.VMEM((columns, dh), BF16),
            pltpu.VMEM((columns, dh), BF16),
            pltpu.VMEM((slots, rows), BF16),
            pltpu.VMEM((held, 2 * rows, columns), F32),
            pltpu.VMEM((held, 2 * rows, columns), BF16),
            pltpu.VMEM((2 * rows, columns), BF16),
            pltpu.VMEM((8, columns), F32),
            pltpu.VMEM((8, columns), F32),
            pltpu.VMEM((dh, columns), F32),
            pltpu.VMEM((dh, columns), F32),
            pltpu.VMEM((2, 2 * rows, dh), F32),
            pltpu.VMEM((held, 2 * rows, dh), F32),
            pltpu.VMEM((held, 2 * rows, dh), BF16),
            pltpu.VMEM((held, 2 * rows, dh), BF16),
            pltpu.VMEM((held, 2 * rows, dh), BF16),
            pltpu.VMEM((held, 2 * rows, dh), BF16),
            pltpu.VMEM(moved, BF16),
            pltpu.VMEM(moved, BF16),
            pltpu.VMEM(moved, BF16),
            pltpu.VMEM(moved, BF16),
        ]
        + [dma((held,))] * 8
        + [dma((n,))] * 4,
        compiler_params=pltpu.CompilerParams(
            collective_id=0, has_side_effects=True, vmem_limit_bytes=40 * 1024 * 1024
        ),
    )(queries, keys, values, out_grad, segment_ids.reshape(1, rows), route)
    if sub != pad_rows:

        def in_rows(block):
            split = block.reshape(n, heads, pad_rows, dh)[:, :, :sub]
            return split.transpose(0, 2, 1, 3).reshape(queries.shape)

        attended, query_grad = in_rows(attended), in_rows(query_grad)
    return attended, query_grad, key_grad, value_grad


def solution(mesh):
    rows = P(("groups", "ctx"), None)
    return jax.shard_map(
        functools.partial(body, mesh.shape["ctx"]),
        mesh=mesh,
        in_specs=(rows, rows, rows, rows, P(("groups", "ctx")), rows),
        out_specs=(rows, rows, rows, rows),
        check_vma=False,
    )
```

```python
import functools

import jax
import jax.numpy as jnp
from jax import lax
from jax.experimental import pallas as pl
from jax.experimental.pallas import tpu as pltpu
from jax.sharding import PartitionSpec as P

MESH = pl.DeviceIdType.MESH
F32 = jnp.float32
BF16 = jnp.bfloat16
big_negative = -1e30
reach = 3 * 512
pad_rows = 8
LANES = 256


def flip(block):
    return block.astype(F32).T.astype(BF16)


def product(left, right):
    return jnp.dot(left, right, preferred_element_type=F32)


def kernel(
    n, heads, factor, back, sub,
    q_hbm, k_hbm, v_hbm, g_hbm, seg_hbm, route_hbm,
    att_ref, dq_ref, kg_ref, vg_ref,
    q_ref, g_ref, seg_ref, route_ref, load_sem,
    kv, q_t, g_t, q_rows, g_rows, perm, score, prob, grad_score, top, total, out_t, dq_t,
    half_terms, own_terms, sib_out, sib_in, part_out, part_in, att_out, dq_out, att_in, dq_in,
    kv_send, kv_recv, fwd_send, fwd_recv, sib_send, sib_recv, part_send, part_recv,
    att_send, att_recv, dq_send, dq_recv,
):
    me = lax.axis_index("ctx")
    chip, core = lax.div(me, 2), lax.rem(me, 2)
    other = 1 - core
    sibling = chip * 2 + other
    chips = n // 2
    rows, dh = k_hbm.shape
    columns = heads * rows
    far = jnp.minimum(chip, back)
    ahead = jnp.minimum(chips - 1 - chip, back)

    loads = [
        pltpu.make_async_copy(source, held, load_sem.at[at])
        for at, (source, held) in enumerate((
            (k_hbm, kv.at[0, core, pl.ds(0, rows)]),
            (v_hbm, kv.at[0, core, pl.ds(rows, rows)]),
            (seg_hbm, seg_ref),
            (route_hbm, route_ref),
            (q_hbm, q_ref),
            (g_hbm, g_ref),
        ))
    ]
    for load in loads:
        load.start()
    barrier = pltpu.get_barrier_semaphore()

    def greet(step, carry):
        pl.semaphore_signal(
            barrier, inc=1, device_id={"ctx": lax.rem(me + step, n)}, device_id_type=MESH
        )
        return carry

    lax.fori_loop(1, n, greet, 0)

    for load in loads[:3]:
        load.wait()
    own_seg = seg_ref[...].astype(F32)
    kv[0, core, pl.ds(2 * rows, 16), :] = jnp.broadcast_to(own_seg, (16, rows)).astype(BF16)
    pl.semaphore_wait(barrier, n - 1)

    def kv_copy(source, step, target):
        return pltpu.make_async_remote_copy(
            src_ref=kv.at[source, core], dst_ref=kv.at[step, core],
            send_sem=kv_send.at[step], recv_sem=kv_recv.at[step],
            device_id={"ctx": target}, device_id_type=MESH,
        )

    def fwd_copy(step, which):
        return pltpu.make_async_remote_copy(
            src_ref=kv.at[step, which], dst_ref=kv.at[step, which],
            send_sem=fwd_send.at[step], recv_sem=fwd_recv.at[step],
            device_id={"ctx": sibling}, device_id_type=MESH,
        )

    def sib_copy(step):
        return pltpu.make_async_remote_copy(
            src_ref=sib_out.at[step], dst_ref=sib_in.at[step],
            send_sem=sib_send.at[step], recv_sem=sib_recv.at[step],
            device_id={"ctx": sibling}, device_id_type=MESH,
        )

    def part_copy(step, target):
        return pltpu.make_async_remote_copy(
            src_ref=part_out.at[step], dst_ref=part_in.at[step],
            send_sem=part_send.at[step], recv_sem=part_recv.at[step],
            device_id={"ctx": target}, device_id_type=MESH,
        )

    def row_copy(outgoing, incoming, sends, recvs, step):
        target = lax.rem(me + step, n)
        return pltpu.make_async_remote_copy(
            src_ref=outgoing.at[target], dst_ref=incoming.at[me],
            send_sem=sends.at[step], recv_sem=recvs.at[step],
            device_id={"ctx": target}, device_id_type=MESH,
        )

    fwd_copy(0, core).start()

    odd = lax.rem(chip, 2)
    partner = me + 2 - 4 * odd
    ahead_even = lax.div(ahead, 2)

    def send_kv(step, carry):
        kv_copy(0, 2 * step, me + 4 * step).start()
        return carry

    lax.fori_loop(1, ahead_even + 1, send_kv, 0)

    def for_partner(step):
        there = step + 1 - 2 * odd
        return there, (lax.rem(step, 2) == 0) & (there >= 0) & (there <= back)

    def relay(step, finished):
        there, needed = for_partner(step)

        @pl.when(needed)
        def _():
            copy = kv_copy(step, there, partner)
            if finished:
                copy.wait_send()
            else:
                copy.start()

    relay(0, False)

    for load in loads[3:]:
        load.wait()
    for h in range(heads):
        part = slice(h * dh, (h + 1) * dh)
        block = slice(h * rows, (h + 1) * rows)
        q_h, g_h = q_ref[:, part], g_ref[:, part]
        q_t[:, block] = flip(q_h)
        g_t[:, block] = flip(g_h)
        q_rows[block, :] = q_h
        g_rows[block, :] = g_h

    slots = n * pad_rows
    spread = (
        lax.shift_right_logical(lax.broadcasted_iota(jnp.int32, (n, slots), 1), 3)
        == lax.broadcasted_iota(jnp.int32, (n, slots), 0)
    )
    routing = jnp.broadcast_to(route_ref[...].astype(F32), (16, n)).astype(BF16)
    block_of = product(routing, jnp.where(spread, 1.0, 0.0).astype(BF16))[:1]
    token = lax.broadcasted_iota(jnp.int32, (rows, slots), 1) & (pad_rows - 1)
    wanted = block_of * float(sub) + token.astype(F32)
    chosen = (wanted == lax.broadcasted_iota(jnp.int32, (rows, slots), 0).astype(F32)) & (token < sub)
    perm[...] = jnp.where(chosen, 1.0, 0.0).T.astype(BF16)

    top[...] = jnp.full_like(top, big_negative)
    prompt = jnp.floor((own_seg + 0.5) * (1.0 / 3.0)) * 3.0
    query_pos = lax.broadcasted_iota(jnp.int32, (rows, rows), 1) + core * rows
    key_row = lax.broadcasted_iota(jnp.int32, (rows, rows), 0)
    chunks = [slice(at, at + LANES) for at in range(0, columns, LANES)]

    def score_half(step, half):
        key_block = kv[step, half, pl.ds(0, rows), :]
        seg_tile = kv[step, half, pl.ds(2 * rows, 16), :].astype(F32)
        key_seg = jnp.broadcast_to(seg_tile[:1], (rows, rows)).T
        key_pos = key_row + (half * rows - step * 2 * rows)
        allowed = (key_pos <= query_pos) & ((key_seg == own_seg) | (key_seg == prompt))
        bias = jnp.where(allowed, 0.0, big_negative)
        bias = jnp.concatenate([bias] * (LANES // rows), axis=1)
        at = pl.ds(pl.multiple_of(half * rows, rows), rows)
        for chunk in chunks:
            values = product(key_block, q_t[:, chunk]) * factor + bias
            score[step, at, chunk] = values
            top[:, chunk] = jnp.maximum(
                top[:, chunk], jnp.max(values.reshape(rows // 8, 8, LANES), axis=0)
            )

    evens = lax.div(far, 2) + 1

    def scores(turn, carry):
        step = jnp.where(turn < evens, 2 * turn, 2 * (turn - evens) + 1)

        @pl.when(step > 0)
        def _():
            kv_copy(0, step, me).wait_recv()
            relay(step, False)
            fwd_copy(step, core).start()

        score_half(step, core)
        fwd_copy(step, other).wait_recv()
        score_half(step, other)
        return carry

    lax.fori_loop(0, far + 1, scores, 0)
    row_top = jnp.max(top[...], axis=0, keepdims=True)
    top[...] = jnp.broadcast_to(row_top, top.shape)
    total[...] = jnp.zeros_like(total)
    out_t[...] = jnp.zeros_like(out_t)
    dq_t[...] = jnp.zeros_like(dq_t)

    def sums(step, carry):
        for at in (pl.ds(0, rows), pl.ds(rows, rows)):
            for chunk in chunks:
                values = jnp.exp(score[step, at, chunk] - top[:1, chunk])
                score[step, at, chunk] = values
                total[:, chunk] += jnp.sum(values.reshape(rows // 8, 8, LANES), axis=0)
        return carry

    lax.fori_loop(0, far + 1, sums, 0)
    total[...] = jnp.broadcast_to(
        1.0 / jnp.sum(total[...], axis=0, keepdims=True), total.shape
    )

    def both(step, first):
        return jnp.concatenate(
            [kv[step, 0, pl.ds(first, rows), :], kv[step, 1, pl.ds(first, rows), :]], axis=0
        )

    def outputs(step, carry):
        value_t = flip(both(step, rows))
        for chunk in chunks:
            values = score[step, :, chunk] * total[:1, chunk]
            score[step, :, chunk] = values
            low = values.astype(BF16)
            prob[step, :, chunk] = low
            out_t[:, chunk] += product(value_t, low)
        return carry

    lax.fori_loop(0, far + 1, outputs, 0)

    def stage(transposed, outgoing, incoming, sends, recvs):
        pieces = []
        for h in range(heads):
            low = transposed[:, h * rows:(h + 1) * rows].astype(BF16)
            moved = lax.dot_general(
                perm[...], low, (((1,), (1,)), ((), ())), preferred_element_type=F32
            )
            pieces.append(moved.reshape(n, pad_rows, dh))
        for h in range(0, heads, 2):
            outgoing[:, h * pad_rows:(h + 2) * pad_rows, :] = jnp.concatenate(
                pieces[h:h + 2], axis=1
            ).astype(BF16)

        def send(step, carry):
            row_copy(outgoing, incoming, sends, recvs, step).start()
            return carry

        lax.fori_loop(1, n, send, 0)
        incoming[me] = outgoing[me]

    stage(out_t, att_out, att_in, att_send, att_recv)
    for chunk in chunks:
        low = out_t[:, chunk].astype(BF16).astype(F32)
        dots = jnp.sum(g_t[:, chunk].astype(F32) * low, axis=0, keepdims=True)
        top[:, chunk] = jnp.broadcast_to(dots, (8, LANES))

    def finish(step):
        sib_copy(step).wait_recv()
        own_terms[step] = own_terms[step] + sib_in[step].astype(F32)

        @pl.when(step > 0)
        def _():
            part_out[step] = own_terms[step].astype(BF16)
            part_copy(step, me - 2 * step).start()

    def grads(turn, carry):
        step = far - turn
        value_block, key_t = both(step, rows), flip(both(step, 0))
        for chunk in chunks:
            grad_prob = product(value_block, g_t[:, chunk])
            low = (score[step, :, chunk] * (grad_prob - top[:1, chunk])).astype(BF16)
            grad_score[:, chunk] = low
            dq_t[:, chunk] += product(key_t, low)
        key_part = product(grad_score[...], q_rows[...])
        value_part = product(prob[step], g_rows[...])
        for half in range(2):
            part = slice(half * rows, (half + 1) * rows)
            half_terms[half, :rows] = key_part[part]
            half_terms[half, rows:] = value_part[part]
        sib_out[step] = half_terms[other].astype(BF16)
        sib_copy(step).start()
        own_terms[step] = half_terms[core]

        @pl.when(turn > 0)
        def _():
            finish(step + 1)

        return carry

    lax.fori_loop(0, far + 1, grads, 0)
    dq_t[...] = dq_t[...] * factor
    stage(dq_t, dq_out, dq_in, dq_send, dq_recv)
    finish(0)

    def collect(incoming, outgoing, sends, recvs, result):
        def arrive(step, carry):
            row_copy(outgoing, incoming, sends, recvs, step).wait_recv()
            return carry

        lax.fori_loop(1, n, arrive, 0)
        if sub == pad_rows:
            for h in range(0, heads, 2):
                two = incoming[:, h * pad_rows:(h + 2) * pad_rows, :].astype(F32)
                for one in range(2):
                    result[:, (h + one) * dh:(h + one + 1) * dh] = (
                        two[:, one * pad_rows:(one + 1) * pad_rows]
                        .reshape(n * pad_rows, dh)
                        .astype(BF16)
                    )
        else:
            result[...] = incoming[...]

        def sent(step, carry):
            row_copy(outgoing, incoming, sends, recvs, step).wait_send()
            return carry

        lax.fori_loop(1, n, sent, 0)

    collect(att_in, att_out, att_send, att_recv, att_ref)

    def gather_part(step, carry):
        part_copy(step, me).wait_recv()
        own_terms[0] = own_terms[0] + part_in[step].astype(F32)
        return carry

    lax.fori_loop(1, ahead + 1, gather_part, 0)
    kg_ref[...] = (own_terms[0, :rows] * factor).astype(BF16)
    vg_ref[...] = own_terms[0, rows:].astype(BF16)
    collect(dq_in, dq_out, dq_send, dq_recv, dq_ref)

    def drain(step, carry):
        relay(step, True)
        fwd_copy(step, core).wait_send()
        sib_copy(step).wait_send()
        return carry

    lax.fori_loop(0, far + 1, drain, 0)

    def drain_kv(step, carry):
        kv_copy(0, 2 * step, me).wait_send()
        return carry

    lax.fori_loop(1, ahead_even + 1, drain_kv, 0)

    def drain_parts(step, carry):
        part_copy(step, me).wait_send()
        return carry

    lax.fori_loop(1, far + 1, drain_parts, 0)


def body(n, queries, keys, values, out_grad, segment_ids, route):
    rows, dh = keys.shape
    heads = queries.shape[1] // dh
    sub = rows // n
    chips = n // 2
    back = -(-(reach - 1) // (2 * rows))
    back = min(back + back % 2, chips - 1)
    columns = heads * rows
    held = back + 1
    slots = n * pad_rows
    moved = (n, heads * pad_rows, dh)
    row_shape = queries.shape if sub == pad_rows else moved
    vmem = pl.BlockSpec(memory_space=pltpu.VMEM)
    dma = pltpu.SemaphoreType.DMA
    attended, query_grad, key_grad, value_grad = pl.pallas_call(
        functools.partial(kernel, n, heads, dh ** -0.5, back, sub),
        out_shape=(
            jax.ShapeDtypeStruct(row_shape, BF16),
            jax.ShapeDtypeStruct(row_shape, BF16),
            jax.ShapeDtypeStruct((rows, dh), BF16),
            jax.ShapeDtypeStruct((rows, dh), BF16),
        ),
        in_specs=[pl.BlockSpec(memory_space=pltpu.HBM)] * 6,
        out_specs=(vmem,) * 4,
        scratch_shapes=[
            pltpu.VMEM(queries.shape, BF16),
            pltpu.VMEM(queries.shape, BF16),
            pltpu.VMEM((1, rows), jnp.int32),
            pltpu.VMEM(route.shape, jnp.int32),
            dma((6,)),
            pltpu.VMEM((held, 2, 2 * rows + 16, dh), BF16),
            pltpu.VMEM((dh, columns), BF16),
            pltpu.VMEM((dh, columns), BF16),
            pltpu.VMEM((columns, dh), BF16),
            pltpu.VMEM((columns, dh), BF16),
            pltpu.VMEM((slots, rows), BF16),
            pltpu.VMEM((held, 2 * rows, columns), F32),
            pltpu.VMEM((held, 2 * rows, columns), BF16),
            pltpu.VMEM((2 * rows, columns), BF16),
            pltpu.VMEM((8, columns), F32),
            pltpu.VMEM((8, columns), F32),
            pltpu.VMEM((dh, columns), F32),
            pltpu.VMEM((dh, columns), F32),
            pltpu.VMEM((2, 2 * rows, dh), F32),
            pltpu.VMEM((held, 2 * rows, dh), F32),
            pltpu.VMEM((held, 2 * rows, dh), BF16),
            pltpu.VMEM((held, 2 * rows, dh), BF16),
            pltpu.VMEM((held, 2 * rows, dh), BF16),
            pltpu.VMEM((held, 2 * rows, dh), BF16),
            pltpu.VMEM(moved, BF16),
            pltpu.VMEM(moved, BF16),
            pltpu.VMEM(moved, BF16),
            pltpu.VMEM(moved, BF16),
        ]
        + [dma((held,))] * 8
        + [dma((n,))] * 4,
        compiler_params=pltpu.CompilerParams(
            collective_id=0, has_side_effects=True, vmem_limit_bytes=40 * 1024 * 1024
        ),
    )(queries, keys, values, out_grad, segment_ids.reshape(1, rows), route)
    if sub != pad_rows:

        def in_rows(block):
            split = block.reshape(n, heads, pad_rows, dh)[:, :, :sub]
            return split.transpose(0, 2, 1, 3).reshape(queries.shape)

        attended, query_grad = in_rows(attended), in_rows(query_grad)
    return attended, query_grad, key_grad, value_grad


def solution(mesh):
    rows = P(("groups", "ctx"), None)
    return jax.shard_map(
        functools.partial(body, mesh.shape["ctx"]),
        mesh=mesh,
        in_specs=(rows, rows, rows, rows, P(("groups", "ctx")), rows),
        out_specs=(rows, rows, rows, rows),
        check_vma=False,
    )
```
